512 devices in a mesh: tok: 16 (over z_hi, y), row: 4 (over x), col: 8 (over z_lo, core).
Axes of the slice: x: 4, y: 8, z: 8 (z_hi: 2, z_lo: 4; z = z_hi * 4 + z_lo), core: 2. Of those that a mesh axis runs over, the one named last changes fastest.
Arguments:
- inputs: bfloat16 [640, 6144], P('tok', 'row'), may hold values from -6 to 6
- pre_act: bfloat16 [640, 49152], P('row', ('tok', 'col')), may hold values from -9 to 9
- w_in: bfloat16 [6144, 49152], P('row', ('tok', 'col')), may hold values from -0.078125 to 0.078125
- w_out: bfloat16 [49152, 6144], P(('tok', 'col'), 'row'), may hold values from -0.02734375 to 0.02734375
- out_grad: bfloat16 [640, 6144], P(('tok', 'col'), 'row'), may hold values from -1.1953125 to 1.1953125
Outputs:
- input_grad: bfloat16 [640, 6144], P(('tok', 'col'), 'row')
- w_in_grad: bfloat16 [6144, 49152], P('row', ('tok', 'col'))
- bias_in_grad: float32 [49152], P(('tok', 'col'))
- w_out_grad: bfloat16 [49152, 6144], P(('tok', 'col'), 'row')
- bias_out_grad: float32 [6144], P('row')
The draws below stay inside these ranges and needn't reach their ends.
All inputs are finite; a program needn't handle non-finite values.
Results may differ from the reference program's by a relative error of at most 0.018.
Values may be sent and summed in bfloat16 or wider, within the bound.
A program may use at most 64 MiB of HBM per device.

```python
import math
import jax
import jax.numpy as jnp
from jax import lax

D = 6144
FF = 49152
TOKENS = 640
N_ROW = 4


def block_scale(stream_key, extent, split, smallest, largest):
    loudness = 1.0
    for axis_at, parts in split:
        draws = jax.random.uniform(jax.random.fold_in(jax.random.fold_in(stream_key, 6), axis_at), (parts,), jnp.float32, smallest / len(split), largest / len(split))
        loudness = loudness * jnp.repeat(jnp.exp(draws), extent[axis_at] // parts).reshape((-1,) + (1,) * (len(extent) - 1 - axis_at))
    return loudness


def centred(stream_key, shape, deviation, bound, shards=(), dtype=jnp.bfloat16):
    loudness = block_scale(stream_key, shape, shards, -0.22, 0.18) if shards else 1.0
    values = jax.random.normal(stream_key, shape, jnp.float32) * deviation * loudness
    return jnp.minimum(jnp.maximum(values, -bound), bound).astype(dtype)


def setup_inputs(seed: int = 0) -> dict:
    keys = jax.random.split(jax.random.key(seed), 6)
    return {
        "inputs": centred(keys[0], (TOKENS, D), 1.0, 6.0, ((0, 16), (1, 4))),
        "pre_act": centred(keys[1], (TOKENS, FF), 1.5, 9.0, ((0, 4), (1, 128))),
        "w_in": centred(keys[2], (D, FF), D ** -0.5, 0.078125, ((0, 4), (1, 128))),
        "w_out": centred(keys[3], (FF, D), FF ** -0.5, 0.02734375, ((0, 128), (1, 4))),
        "out_grad": centred(keys[4], (TOKENS, D), 0.2, 1.1953125, ((0, 128), (1, 4))),
    }


root_two_pi = math.sqrt(2.0 / math.pi)

def gelu_parts(values):
    cubic = values * values * values
    inner = root_two_pi * (values + 0.044715 * cubic)
    tangent = jnp.tanh(inner)
    result = 0.5 * values * (1.0 + tangent)
    slope = 0.5 * (1.0 + tangent) + 0.5 * values * (1.0 - tangent * tangent) * root_two_pi * (1.0 + 3.0 * 0.044715 * values * values)
    return (result, slope)

def reference(inputs, pre_act, w_in, w_out, out_grad):
    result, slope = gelu_parts(pre_act.astype(jnp.float32))
    hidden = result.astype(jnp.bfloat16)
    w_out_grad = jnp.dot(hidden.T, out_grad, preferred_element_type=jnp.float32).astype(jnp.bfloat16)
    bias_out_grad = lax.optimization_barrier(jnp.sum(out_grad.astype(jnp.float32), axis=0))
    group = D // N_ROW
    hidden_grad = jnp.zeros((TOKENS, FF), jnp.float32)
    for index in range(N_ROW):
        part = jnp.dot(out_grad[:, index * group:(index + 1) * group], w_out[:, index * group:(index + 1) * group].T, preferred_element_type=jnp.float32)
        part = lax.optimization_barrier(part.astype(jnp.bfloat16)).astype(jnp.float32)
        hidden_grad = hidden_grad + part
    act_grad = (hidden_grad * slope).astype(jnp.bfloat16)
    bias_in_grad = lax.optimization_barrier(jnp.sum(act_grad.astype(jnp.float32), axis=0))
    w_in_grad = jnp.dot(inputs.T, act_grad, preferred_element_type=jnp.float32).astype(jnp.bfloat16)
    input_grad = jnp.dot(act_grad, w_in.T, preferred_element_type=jnp.float32).astype(jnp.bfloat16)
    return (input_grad, w_in_grad, bias_in_grad, w_out_grad, bias_out_grad)
```

```python
import functools
import math

import jax
import jax.numpy as jnp
import numpy as np
from jax import lax
from jax.experimental import pallas as pl
from jax.experimental.pallas import tpu as pltpu
from jax.sharding import PartitionSpec as P

MESH = pl.DeviceIdType.MESH
F32 = jnp.float32
BF16 = jnp.bfloat16
root_two_pi = math.sqrt(2.0 / math.pi)
T = 5
ZL = 4
STEPS = 3


def gelu_parts(values):
    cubic = values * values * values
    inner = root_two_pi * (values + 0.044715 * cubic)
    tangent = jnp.tanh(inner)
    result = 0.5 * values * (1.0 + tangent)
    slope = 0.5 * (1.0 + tangent) + 0.5 * values * (1.0 - tangent * tangent) * root_two_pi * (
        1.0 + 3.0 * 0.044715 * values * values
    )
    return (result, slope)


def nt(a, b):
    return lax.dot_general(a, b, (((1,), (1,)), ((), ())), preferred_element_type=F32)


def tn(a, b):
    return lax.dot_general(a, b, (((0,), (0,)), ((), ())), preferred_element_type=F32)


def nn(a, b):
    return lax.dot_general(a, b, (((1,), (0,)), ((), ())), preferred_element_type=F32)


def kernel(
    cfg,
    x_ref, pre_hbm, w_in_hbm, w_out_hbm, og_ref, swap_hbm, unfold_hbm, fold_hbm,
    ig_ref, wi_hbm, bi_ref, wo_hbm, bo_ref,
    w_in, w_out, swap, unfold, fold, sb, rb, gg, ii, gy, pre, hid, slope, pb, pr, act, actz, sx, sr, sc, tb, tr,
    fb, qq, wi, wo,
    loc, outs, s_pre, r_pre, s1, r1, sg, rg, si, ri, sp, rp, sa, ra, ss, rs, st, rt, sq, rq,
):
    N, X, zl_n = cfg["N"], cfg["X"], cfg["ZL"]
    U = 2 * N * T
    H = cfg["H"]
    W = cfg["W"]
    HF = STEPS * W
    M = N * U
    RB = M // X
    UR = RB // U
    TK = 2 * zl_n * T

    tok, x, col = lax.axis_index("tok"), lax.axis_index("row"), lax.axis_index("col")
    y, c = lax.rem(tok, N), lax.rem(col, 2)
    z = (tok // N) * zl_n + col // 2
    b = y + c * (z - y)
    a = z + c * (y - z)

    def dev(yy, zz, cc, xx=x):
        return ((zz // zl_n) * N + yy, xx, lax.rem(zz, zl_n) * 2 + cc)

    def bdev(bb):
        return dev(y + (1 - c) * (bb - y), z + c * (bb - z), c)

    def adev(aa, cc):
        return dev(y + c * (aa - y), z + (1 - c) * (aa - z), cc)

    mate = dev(y, z, 1 - c)

    def rcopy(src, dst, ssem, rsem, to):
        return pltpu.make_async_remote_copy(
            src_ref=src, dst_ref=dst, send_sem=ssem, recv_sem=rsem, device_id=to, device_id_type=MESH
        )

    def got(dst, rsem):
        rcopy(dst, dst, rsem, rsem, mate).wait_recv()

    def sent(src, ssem):
        rcopy(src, src, ssem, ssem, mate).wait_send()

    loads = [
        pltpu.make_async_copy(unfold_hbm, unfold, loc.at[0]),
        pltpu.make_async_copy(pre_hbm, pre.at[x], loc.at[1]),
        pltpu.make_async_copy(swap_hbm, swap, loc.at[2]),
        pltpu.make_async_copy(w_out_hbm, w_out, loc.at[3]),
        pltpu.make_async_copy(w_in_hbm, w_in, loc.at[4]),
        pltpu.make_async_copy(fold_hbm, fold, loc.at[5]),
    ]
    for load in loads:
        load.start()

    bar = pltpu.get_barrier_semaphore()

    def greet(yy, zz, cc, xx=x):
        pl.semaphore_signal(bar, inc=1, device_id=dev(yy, zz, cc, xx), device_id_type=MESH)

    greet(y, z, 1 - c)
    for d in range(1, X):
        greet(y, z, c, lax.rem(x + d, X))

    def greet_step(d, _):
        yy, zz = lax.rem(y + d, N), lax.rem(z + d, N)
        for cc in range(2):
            greet(yy, z, cc)
            greet(y, zz, cc)
        return 0

    lax.fori_loop(1, N, greet_step, 0)

    og = og_ref[...].astype(F32)
    xall = x_ref[...].astype(F32)
    xs = xall[0:T]
    for k in range(1, 2 * zl_n):
        xs = jnp.where(col == k, xall[T * k : T * k + T], xs)
    pad = jnp.zeros((1, W), F32)
    for h in range(2):
        rows = []
        for v in (og, xs):
            rows += [v[:, h * HF + j * W : h * HF + (j + 1) * W] for j in range(STEPS)] + [pad]
        sb[h] = jnp.concatenate(rows, axis=0).astype(BF16)

    pl.semaphore_wait(bar, 1 + (X - 1) + 4 * (N - 1))

    @pl.when(c == 0)
    def _():
        rb[2 * z] = sb[0]
        rcopy(sb.at[1], rb.at[2 * y], s1.at[0], r1.at[0], mate).start()

    @pl.when(c == 1)
    def _():
        rb[2 * y + 1] = sb[1]
        rcopy(sb.at[0], rb.at[2 * z + 1], s1.at[0], r1.at[0], mate).start()

    def small(d, _):
        yy, zz = lax.rem(y + d, N), lax.rem(z + d, N)
        rcopy(sb.at[0], rb.at[2 * z + c], s1.at[0], r1.at[0], dev(y, zz, 0)).start()
        rcopy(sb.at[1], rb.at[2 * y + c], s1.at[0], r1.at[0], dev(yy, z, 1)).start()
        return 0

    lax.fori_loop(1, N, small, 0)

    for d in range(1, X):
        rcopy(pre_hbm, pre.at[x], s_pre.at[0], r_pre.at[0], dev(y, z, c, lax.rem(x + d, X))).start()

    loads[0].wait()
    got(rb.at[pl.ds(0, 2 * N - 1)], r1.at[0])
    unit = nn(unfold[...], rb[...].reshape(2 * N * 32, W))
    own = c * N + b
    for k, buf in enumerate((gg, ii)):
        for j in range(STEPS):
            at = (k * STEPS + j) * U
            buf[own, :, j * W : (j + 1) * W] = unit[at : at + U].astype(BF16)

    for buf, ssem, rsem in ((gg, sg, rg), (ii, si, ri)):

        def large(d, _, buf=buf, ssem=ssem, rsem=rsem):
            bb = lax.rem(b + d, N)
            rcopy(buf.at[own], buf.at[own], ssem.at[0], rsem.at[own], bdev(bb)).start()
            return 0

        lax.fori_loop(1, N, large, 0)
        rcopy(buf.at[own], buf.at[own], ssem.at[0], rsem.at[own], mate).start()

    loads[1].wait()
    got(pre.at[pl.ds(0, X - 1)], r_pre.at[0])
    for r in range(X):
        for q in range(RB // TK):
            g = r * (RB // TK) + q
            zh, yy = g // N, g % N
            at = yy * U + zh * TK
            result, grade = gelu_parts(pre[r].astype(F32)[q * TK : q * TK + TK])
            hid[at : at + TK] = result
            slope[at : at + TK] = grade

    def forward(buf, ssem, rsem):
        def step(d, _):
            at = c * N + lax.rem(b + d, N)
            got(buf.at[at], rsem.at[at])
            rcopy(buf.at[at], buf.at[at], ssem.at[0], rsem.at[at], mate).start()
            return 0

        lax.fori_loop(1, N, step, 0)

    def from_mate(buf, rsem):
        def step(k, _):
            at = (1 - c) * N + k
            got(buf.at[at], rsem.at[at])
            return 0

        lax.fori_loop(0, N, step, 0)

    forward(gg, sg, rg)
    loads[2].wait()
    loads[3].wait()
    from_mate(gg, rg)

    for d in range(1, X + 1):
        r = lax.rem(x + d, X)
        g1 = gg[pl.ds(N, N)].reshape(M, HF)
        mine = pl.ds(pl.multiple_of(r * RB, 16), RB)
        g1y = nn(swap[mine], g1).astype(BF16)
        gy[mine] = g1y
        g0 = gg[pl.ds(r * UR, UR)].reshape(RB, HF)
        part = nt(g0, w_out[:, :HF]) + nt(g1y, w_out[:, HF:])
        if d < X:
            pb[r] = part.astype(BF16)
            rcopy(pb.at[r], pr.at[x], sp.at[0], rp.at[0], dev(y, z, c, r)).start()
        else:
            pr[x] = part.astype(BF16)

    forward(ii, si, ri)

    hidden = hid[...].astype(BF16)
    wo[:, :HF] = tn(hidden, gg[pl.ds(0, N)].reshape(M, HF)).astype(BF16)
    bo = [jnp.sum(gg[pl.ds(0, N)].reshape(M, HF).astype(F32), axis=0, keepdims=True)]
    wo[:, HF:] = tn(hidden, gy[...]).astype(BF16)
    bo += [jnp.sum(gy[...].astype(F32), axis=0, keepdims=True)]
    bo_ref[...] = jnp.concatenate(bo, axis=1)
    put_wo = pltpu.make_async_copy(wo, wo_hbm, outs.at[0])
    put_wo.start()

    got(pr.at[pl.ds(0, X - 1)], rp.at[0])
    total = pr[0].astype(F32)
    for r in range(1, X):
        total = total + pr[r].astype(F32)
    mine = pl.ds(pl.multiple_of(x * RB, 16), RB)
    act[x] = (total * slope[mine]).astype(BF16)
    for d in range(1, X):
        rcopy(act.at[x], act.at[x], sa.at[0], ra.at[0], dev(y, z, c, lax.rem(x + d, X))).start()

    loads[4].wait()
    loads[5].wait()
    got(act.at[pl.ds(0, X - 1)], ra.at[0])
    acty = act[...].reshape(M, H)
    actz[0] = acty
    actz[1] = nn(swap[...], acty).astype(BF16)

    mate_b = z + c * (y - z)
    for i in range(X):
        k = lax.rem(mate_b // UR + i, X)
        rows = pl.ds(pl.multiple_of(k * RB, 16), RB)
        part = nt(actz[1 - c, rows], w_in[1 - c]).astype(BF16)
        sx[pl.ds(k * UR, UR)] = part.reshape(UR, U, HF)
        rcopy(sx.at[pl.ds(k * UR, UR)], sr.at[pl.ds(k * UR, UR)], ss.at[0], rs.at[k], mate).start()

    bi_ref[...] = jnp.sum(acty.astype(F32), axis=0, keepdims=True)

    for i in range(X):
        k = lax.rem(b // UR + i, X)
        rows = pl.ds(pl.multiple_of(k * RB, 16), RB)
        part = nt(actz[c, rows], w_in[c])
        got(sr.at[pl.ds(k * UR, UR)], rs.at[k])
        part = part.reshape(UR, U, HF) + sr[pl.ds(k * UR, UR)].astype(F32)
        sc[pl.ds(k * UR, UR)] = part
        tb[pl.ds(k * UR, UR)] = part.astype(BF16)
        for u in range(UR):
            bb = k * UR + u

            @pl.when(bb != b)
            def _(bb=bb):
                rcopy(tb.at[bb], tr.at[b], st.at[0], rt.at[0], bdev(bb)).start()

    from_mate(ii, ri)
    for h in range(2):
        wi[h] = tn(ii[pl.ds(h * N, N)].reshape(M, HF), actz[h]).astype(BF16)
    put_wi = pltpu.make_async_copy(wi, wi_hbm, outs.at[1])
    put_wi.start()

    got(tr.at[pl.ds(0, N - 1)], rt.at[0])
    total = sc[b]
    for d in range(1, N):
        total = total + tr[lax.rem(b + d, N)].astype(F32)
    total = total.astype(BF16)
    stack = jnp.concatenate([total[:, j * W : (j + 1) * W] for j in range(STEPS)], axis=0)
    fb[...] = nn(fold[...], stack).astype(BF16).reshape(2 * N, 16, W)
    qq[own_slot(c, a, N)] = fb[2 * a + c]
    rcopy(fb.at[2 * a + 1 - c], qq.at[own_slot(c, a, N)], sq.at[0], rq.at[0], mate).start()

    def last(d, _):
        aa = lax.rem(a + d, N)
        for k in range(2):
            cc = lax.rem(c + k, 2)
            rcopy(fb.at[2 * aa + cc], qq.at[own_slot(c, a, N)], sq.at[0], rq.at[0], adev(aa, cc)).start()
        return 0

    lax.fori_loop(1, N, last, 0)
    got(qq.at[pl.ds(0, 2 * N - 1)], rq.at[0])
    for h in range(2):
        rows = jnp.sum(qq[pl.ds(h * N, N)].astype(F32), axis=0)
        for j in range(STEPS):
            at = h * HF + j * W
            ig_ref[:, at : at + W] = rows[T * j : T * j + T].astype(BF16)

    sent(rb.at[pl.ds(0, 2 * N - 1)], s1.at[0])
    sent(pre.at[pl.ds(0, X - 1)], s_pre.at[0])
    sent(gg.at[pl.ds(0, 2 * N - 1)], sg.at[0])
    sent(ii.at[pl.ds(0, 2 * N - 1)], si.at[0])
    sent(pb.at[pl.ds(0, X - 1)], sp.at[0])
    sent(act.at[pl.ds(0, X - 1)], sa.at[0])
    sent(sx, ss.at[0])
    sent(tb.at[pl.ds(0, N - 1)], st.at[0])
    sent(qq.at[pl.ds(0, 2 * N - 1)], sq.at[0])
    put_wo.wait()
    put_wi.wait()


def own_slot(c, a, n):
    return c * n + a


def tables(n, u):
    m = n * u
    q = 2 * T
    r = np.arange(m)
    swap = np.zeros((m, m), np.float32)
    swap[r, ((r % u) // q) * u + (r // u) * q + r % q] = 1
    unfold = np.zeros((2 * STEPS * u, 2 * n * 32), np.float32)
    fold = np.zeros((2 * n * 16, STEPS * u), np.float32)
    for j in range(STEPS):
        for t in range(u):
            for k in range(2):
                unfold[(k * STEPS + j) * u + t, (t // T) * 32 + k * 16 + T * j + t % T] = 1
            fold[(t // T) * 16 + T * j + t % T, j * u + t] = 1
    return swap, unfold, fold


def solution(mesh):
    X = mesh.shape["row"]
    zl_n = mesh.shape["col"] // 2
    N = math.isqrt(mesh.shape["tok"] * zl_n)
    U = 2 * N * T
    M = N * U

    def body(inputs, pre_act, w_in, w_out, out_grad):
        F, H = w_in.shape
        W = F // (2 * STEPS)
        HF = F // 2
        RB = M // X
        cfg = {"N": N, "X": X, "ZL": zl_n, "H": H, "W": W}
        consts = [jnp.asarray(t, BF16) for t in tables(N, U)]
        vm = pl.BlockSpec(memory_space=pltpu.VMEM)
        hbm = pl.BlockSpec(memory_space=pl.ANY)
        dma = pltpu.SemaphoreType.DMA
        outs = pl.pallas_call(
            functools.partial(kernel, cfg),
            out_shape=(
                jax.ShapeDtypeStruct((T, F), BF16),
                jax.ShapeDtypeStruct((2, HF, H), BF16),
                jax.ShapeDtypeStruct((1, H), F32),
                jax.ShapeDtypeStruct((H, F), BF16),
                jax.ShapeDtypeStruct((1, F), F32),
            ),
            in_specs=[vm, hbm, hbm, hbm, vm, hbm, hbm, hbm],
            out_specs=(vm, hbm, vm, hbm, vm),
            scratch_shapes=[
                pltpu.VMEM((2, HF, H), BF16),
                pltpu.VMEM((H, F), BF16),
                pltpu.VMEM(consts[0].shape, BF16),
                pltpu.VMEM(consts[1].shape, BF16),
                pltpu.VMEM(consts[2].shape, BF16),
                pltpu.VMEM((2, 32, W), BF16),
                pltpu.VMEM((2 * N, 32, W), BF16),
                pltpu.VMEM((2 * N, U, HF), BF16),
                pltpu.VMEM((2 * N, U, HF), BF16),
                pltpu.VMEM((M, HF), BF16),
                pltpu.VMEM((X, RB, H), BF16),
                pltpu.VMEM((M, H), F32),
                pltpu.VMEM((M, H), F32),
                pltpu.VMEM((X, RB, H), BF16),
                pltpu.VMEM((X, RB, H), BF16),
                pltpu.VMEM((X, RB, H), BF16),
                pltpu.VMEM((2, M, H), BF16),
                pltpu.VMEM((N, U, HF), BF16),
                pltpu.VMEM((N, U, HF), BF16),
                pltpu.VMEM((N, U, HF), F32),
                pltpu.VMEM((N, U, HF), BF16),
                pltpu.VMEM((N, U, HF), BF16),
                pltpu.VMEM((2 * N, 16, W), BF16),
                pltpu.VMEM((2 * N, 16, W), BF16),
                pltpu.VMEM((2, HF, H), BF16),
                pltpu.VMEM((H, F), BF16),
                dma((6,)), dma((2,)),
                dma((1,)), dma((1,)),
                dma((1,)), dma((1,)),
                dma((1,)), dma((2 * N,)),
                dma((1,)), dma((2 * N,)),
                dma((1,)), dma((1,)),
                dma((1,)), dma((1,)),
                dma((1,)), dma((X,)),
                dma((1,)), dma((1,)),
                dma((1,)), dma((1,)),
            ],
            compiler_params=pltpu.CompilerParams(
                collective_id=0, has_side_effects=True, vmem_limit_bytes=60 * 1024 * 1024
            ),
        )(inputs, pre_act, w_in.reshape(2, HF, H), w_out, out_grad, *consts)
        ig, wi, bi, wo, bo = outs
        return (ig, wi.reshape(F, H), bi.reshape(H), wo, bo.reshape(F))

    return jax.shard_map(
        body,
        mesh=mesh,
        in_specs=(
            P("tok", "row"),
            P("row", ("tok", "col")),
            P("row", ("tok", "col")),
            P(("tok", "col"), "row"),
            P(("tok", "col"), "row"),
        ),
        out_specs=(
            P(("tok", "col"), "row"),
            P("row", ("tok", "col")),
            P(("tok", "col")),
            P(("tok", "col"), "row"),
            P("row"),
        ),
        check_vma=False,
    )
```

```python
import functools
import math

import jax
import jax.numpy as jnp
import numpy as np
from jax import lax
from jax.experimental import pallas as pl
from jax.experimental.pallas import tpu as pltpu
from jax.sharding import PartitionSpec as P

MESH = pl.DeviceIdType.MESH
F32 = jnp.float32
BF16 = jnp.bfloat16
root_two_pi = math.sqrt(2.0 / math.pi)
T = 5
ZL = 4
CHUNKS = 2
VM = 60 * 2**20
STEPS = 3


def gelu_parts(values):
    cubic = values * values * values
    inner = root_two_pi * (values + 0.044715 * cubic)
    tangent = jnp.tanh(inner)
    result = 0.5 * values * (1.0 + tangent)
    slope = 0.5 * (1.0 + tangent) + 0.5 * values * (1.0 - tangent * tangent) * root_two_pi * (
        1.0 + 3.0 * 0.044715 * values * values
    )
    return (result, slope)


def nt(a, b):
    return lax.dot_general(a, b, (((1,), (1,)), ((), ())), preferred_element_type=F32)


def tn(a, b):
    return lax.dot_general(a, b, (((0,), (0,)), ((), ())), preferred_element_type=F32)


def nn(a, b):
    return lax.dot_general(a, b, (((1,), (0,)), ((), ())), preferred_element_type=F32)


class Gather:
    def __init__(self, n, me, buf, slot, pieces, ssem, rsem, send, mate):
        self.n, self.me, self.buf, self.slot, self.pieces = n, me, buf, slot, pieces
        self.ssem, self.rsem, self.send, self.mate = ssem, rsem, send, mate

    def piece(self, unit, p):
        at, size = self.pieces[p]
        return self.buf.at[self.slot(unit), pl.ds(at, size)], self.rsem.at[self.slot(unit) * len(self.pieces) + p]

    def push(self, unit, p, to):
        ref, sem = self.piece(unit, p)
        self.send(ref, ref, self.ssem.at[0], sem, to).start()

    def of(self, way, far):
        half = (len(self.pieces) + 1) // 2
        every = range(len(self.pieces))
        return every if not far else (every[:half] if way > 0 else every[half:])

    def start(self):
        for p in range(len(self.pieces)):
            for way in (1, -1):
                if p in self.of(way, self.n == 2):
                    self.push(self.me, p, way)
        if self.mate:
            for p in range(len(self.pieces)):
                self.push(self.me, p, 0)

    def step(self, k):
        for p in range(len(self.pieces)):
            for way in (1, -1):
                if p in self.of(way, 2 * k == self.n):
                    unit = lax.rem(self.me - way * k + self.n, self.n)
                    ref, sem = self.piece(unit, p)
                    self.send(ref, ref, sem, sem, 0).wait_recv()
                    if 2 * k < self.n and p in self.of(way, 2 * k + 2 == self.n):
                        self.push(unit, p, way)
                    if self.mate:
                        self.push(unit, p, 0)


class Scatter:
    def __init__(self, n, me, own, out, land, pieces, ssem, rsem, send):
        self.n, self.me, self.own, self.out, self.land, self.pieces = n, me, own, out, land, pieces
        self.ssem, self.rsem, self.send = ssem, rsem, send

    def of(self, way, first):
        half = (len(self.pieces) + 1) // 2
        every = range(len(self.pieces))
        return every if not first else (every[:half] if way > 0 else every[half:])

    def place(self, way, s, p):
        at = (0 if way > 0 else self.n // 2) + s
        rows = pl.ds(*self.pieces[p])
        return self.out.at[at, rows], self.land.at[at, rows], self.rsem.at[at * len(self.pieces) + p]

    def arrived(self, way, s, p):
        _, land, sem = self.place(way, s, p)
        self.send(land, land, sem, sem, 0).wait_recv()
        return land[...].astype(F32)

    def step(self, s):
        for p in range(len(self.pieces)):
            for way in (1, -1):
                if p in self.of(way, s == 0):
                    unit = lax.rem(self.me + way * (self.n // 2 - s) + self.n, self.n)
                    value = self.own[unit, pl.ds(*self.pieces[p])]
                    if s and p in self.of(way, s == 1):
                        value = value + self.arrived(way, s - 1, p)
                    out, land, sem = self.place(way, s, p)
                    out[...] = value.astype(BF16)
                    self.send(out, land, self.ssem.at[0], sem, way).start()

    def result(self):
        rows = []
        for p in range(len(self.pieces)):
            value = self.own[self.me, pl.ds(*self.pieces[p])]
            for way in (1, -1):
                if p in self.of(way, self.n == 2):
                    value = value + self.arrived(way, self.n // 2 - 1, p)
            rows.append(value)
        return jnp.concatenate(rows, axis=0)


def kernel(
    cfg,
    x_hbm, pre_hbm, w_in_hbm, w_out_hbm, og_hbm, swap_hbm, unfold_hbm, fold_hbm,
    ig_hbm, wi_hbm, bi_hbm, wo_hbm, bo_hbm,
    x_ref, og_ref, ig_ref, wi, bi_ref, wo, bo_ref,
    w_in, w_out, swap, unfold, fold, sb, rb, gg, ii, gy, pre, hid, slope, pb, pr, act, actz, sx, sr, sc, tb, tr,
    fb, qq,
    loc, outs, s_pre, r_pre, s1, r1, sg, rg, si, ri, sp, rp, sa, ra, ss, rs, st, rt, sq, rq,
):
    N, X, zl_n = cfg["N"], cfg["X"], cfg["ZL"]
    U = 2 * N * T
    H = cfg["H"]
    W = cfg["W"]
    HF = STEPS * W
    M = N * U
    RB = M // X
    UR = RB // U
    TK = 2 * zl_n * T

    tok, x, col = lax.axis_index("tok"), lax.axis_index("row"), lax.axis_index("col")
    y, c = lax.rem(tok, N), lax.rem(col, 2)
    z = (tok // N) * zl_n + col // 2
    b = y + c * (z - y)
    a = z + c * (y - z)

    def dev(yy, zz, cc, xx=x):
        return ((zz // zl_n) * N + yy, xx, lax.rem(zz, zl_n) * 2 + cc)

    def bdev(bb):
        return dev(y + (1 - c) * (bb - y), z + c * (bb - z), c)

    def adev(aa, cc):
        return dev(y + c * (aa - y), z + (1 - c) * (aa - z), cc)

    def xdev(xx):
        return dev(y, z, c, xx)

    mate = dev(y, z, 1 - c)

    def rcopy(src, dst, ssem, rsem, to):
        return pltpu.make_async_remote_copy(
            src_ref=src, dst_ref=dst, send_sem=ssem, recv_sem=rsem, device_id=to, device_id_type=MESH
        )

    def along_b(src, dst, ssem, rsem, way):
        to = mate if way == 0 else bdev(lax.rem(b + way + N, N))
        return rcopy(src, dst, ssem, rsem, to)

    def along_x(src, dst, ssem, rsem, way):
        return rcopy(src, dst, ssem, rsem, xdev(lax.rem(x + way + X, X)))

    def got(dst, rsem):
        rcopy(dst, dst, rsem, rsem, mate).wait_recv()

    def sent(src, ssem):
        rcopy(src, src, ssem, ssem, mate).wait_send()

    loads = [
        pltpu.make_async_copy(pre_hbm, pre.at[x], loc.at[0]),
        pltpu.make_async_copy(unfold_hbm, unfold, loc.at[1]),
        pltpu.make_async_copy(swap_hbm, swap, loc.at[2]),
        pltpu.make_async_copy(w_out_hbm, w_out, loc.at[3]),
        pltpu.make_async_copy(w_in_hbm, w_in, loc.at[4]),
        pltpu.make_async_copy(fold_hbm, fold, loc.at[5]),
    ]
    tokens = (pltpu.make_async_copy(og_hbm, og_ref, loc.at[6]), pltpu.make_async_copy(x_hbm, x_ref, loc.at[7]))
    for load in tokens:
        load.start()

    stores = []

    def put(src, dst):
        stores.append(pltpu.make_async_copy(src, dst, outs.at[len(stores)]))
        stores[-1].start()

    bar = pltpu.get_barrier_semaphore()

    def greet(yy, zz, cc, xx=x):
        pl.semaphore_signal(bar, inc=1, device_id=dev(yy, zz, cc, xx), device_id_type=MESH)

    greet(y, z, 1 - c)
    for d in range(1, X):
        greet(y, z, c, lax.rem(x + d, X))

    def greet_step(d, _):
        yy, zz = lax.rem(y + d, N), lax.rem(z + d, N)
        for cc in range(2):
            greet(yy, z, cc)
            greet(y, zz, cc)
        return 0

    lax.fori_loop(1, N, greet_step, 0)

    for load in loads:
        load.start()

    for load in tokens:
        load.wait()
    og = og_ref[...].astype(F32)
    xall = x_ref[...].astype(F32)
    xs = xall[0:T]
    for k in range(1, 2 * zl_n):
        xs = jnp.where(col == k, xall[T * k : T * k + T], xs)
    pad = jnp.zeros((1, W), F32)
    for k, v in enumerate((og, xs)):
        for h in range(2):
            rows = [v[:, h * HF + j * W : h * HF + (j + 1) * W] for j in range(STEPS)] + [pad]
            sb[k, h] = jnp.concatenate(rows, axis=0).astype(BF16)

    pl.semaphore_wait(bar, 1 + (X - 1) + 4 * (N - 1))

    def small_phase(k):
        @pl.when(c == 0)
        def _():
            rb[k, 2 * z] = sb[k, 0]
            rcopy(sb.at[k, 1], rb.at[k, 2 * y], s1.at[k], r1.at[k], mate).start()

        @pl.when(c == 1)
        def _():
            rb[k, 2 * y + 1] = sb[k, 1]
            rcopy(sb.at[k, 0], rb.at[k, 2 * z + 1], s1.at[k], r1.at[k], mate).start()

        def small(d, _):
            yy, zz = lax.rem(y + d, N), lax.rem(z + d, N)
            rcopy(sb.at[k, 0], rb.at[k, 2 * z + c], s1.at[k], r1.at[k], dev(y, zz, 0)).start()
            rcopy(sb.at[k, 1], rb.at[k, 2 * y + c], s1.at[k], r1.at[k], dev(yy, z, 1)).start()
            return 0

        lax.fori_loop(1, N, small, 0)

    def unit_of(k, buf):
        got(rb.at[k, pl.ds(0, 2 * N - 1)], r1.at[k])
        unit = nn(unfold[...], rb[k].reshape(2 * N * 16, W)).astype(BF16)
        for j in range(STEPS):
            buf[c * N + b, :, j * W : (j + 1) * W] = unit[j * U : j * U + U]

    small_phase(0)

    for d in range(1, X):
        rcopy(pre_hbm, pre.at[x], s_pre.at[0], r_pre.at[x], xdev(lax.rem(x + d, X))).start()

    def gelu_block(r):
        for q in range(RB // TK):
            g = r * (RB // TK) + q
            zh, yy = g // N, lax.rem(g, N)
            rows = pl.ds(pl.multiple_of(yy * U + zh * TK, 8), TK)
            result, grade = gelu_parts(pre[r].astype(F32)[q * TK : q * TK + TK])
            hid[rows] = result
            slope[rows] = grade

    loads[0].wait()
    gelu_block(x)
    loads[1].wait()
    pieces = cfg["pieces"]
    grads = Gather(N, b, gg, lambda u: c * N + u, pieces, sg, rg, along_b, True)
    xs_ring = Gather(N, b, ii, lambda u: c * N + u, pieces, si, ri, along_b, True)
    unit_of(0, gg)
    grads.start()
    small_phase(1)

    def from_mate(ring):
        def step(k, _):
            for p in range(len(pieces)):
                at = (1 - c) * N + k
                got(ring.buf.at[at, pl.ds(*pieces[p])], ring.rsem.at[at * len(pieces) + p])
            return 0

        lax.fori_loop(0, N, step, 0)

    for k in range(1, N // 2 + 1):
        grads.step(k)
        if k < X:
            r = lax.rem(x + k, X)
            got(pre.at[r], r_pre.at[r])
            gelu_block(r)
    for k in range(N // 2 + 1, X):
        r = lax.rem(x + k, X)
        got(pre.at[r], r_pre.at[r])
        gelu_block(r)
    unit_of(1, ii)
    xs_ring.start()
    for load in loads[2:]:
        load.wait()
    from_mate(grads)

    def part(r):
        g1 = gg[pl.ds(N, N)].reshape(M, HF)
        mine = pl.ds(pl.multiple_of(r * RB, 16), RB)
        g1y = nn(swap[mine], g1).astype(BF16)
        gy[mine] = g1y
        g0 = gg[pl.ds(r * UR, UR)].reshape(RB, HF)
        return nt(g0, w_out[:, :HF]) + nt(g1y, w_out[:, HF:])

    def steps(n, me):
        return [n // 2] + [v for s in range(1, n // 2) for v in (n // 2 - s, n // 2 + s)] + [0]

    later = list(range(1, N // 2 + 1))

    def more():
        if later:
            xs_ring.step(later.pop(0))

    CH = RB // CHUNKS
    for v in steps(X, x)[:-1]:
        r = lax.rem(x + v, X)
        value = part(r).astype(BF16)
        for q in range(CHUNKS):
            pb[q, r] = value[q * CH : q * CH + CH]
            rcopy(pb.at[q, r], pr.at[q, x], sp.at[0], rp.at[q], xdev(r)).start()
    mine = part(x)

    hidden = hid[...].astype(BF16)
    more()
    wo[:, :HF] = tn(hidden, gg[pl.ds(0, N)].reshape(M, HF)).astype(BF16)
    for q in range(CHUNKS):
        got(pr.at[q, pl.ds(0, X - 1)], rp.at[q])
        total = mine[q * CH : q * CH + CH]
        for v in range(1, X):
            total = total + pr[q, lax.rem(x + v, X)].astype(F32)
        rows = pl.ds(pl.multiple_of(x * RB + q * CH, 16), CH)
        act[x, q * CH : q * CH + CH] = (total * slope[rows]).astype(BF16)
        piece = act.at[x, pl.ds(q * CH, CH)]
        for v in steps(X, x)[:-1]:
            rcopy(piece, piece, sa.at[0], ra.at[0], xdev(lax.rem(x + v, X))).start()
    more()
    wo[:, HF:] = tn(hidden, gy[...]).astype(BF16)
    put(wo, wo_hbm)
    got(act.at[pl.ds(0, X - 1)], ra.at[0])
    acty = act[...].reshape(M, H)
    actz[0] = acty.reshape(N, U, H)
    actz[1] = nn(swap[...], acty).astype(BF16).reshape(N, U, H)
    more()

    mate_b = z + c * (y - z)
    order = steps(N, b)
    pairs = [order[i : i + 2] for i in range(0, N, 2)]

    def product(h, base, pair):
        units = [lax.rem(base + v, N) for v in pair]
        rows = jnp.concatenate([actz[h, u] for u in units], axis=0)
        return units, nt(rows, w_in[h])

    def for_mate(i):
        units, value = product(1 - c, mate_b, pairs[i])
        for k, u in enumerate(units):
            sx[u] = value[k * U : k * U + U].astype(BF16)
            rcopy(sx.at[u], sr.at[u], ss.at[0], rs.at[u], mate).start()

    def for_me(i):
        units, value = product(c, b, pairs[i])
        for k, u in enumerate(units):
            got(sr.at[u], rs.at[u])
            sc[u] = value[k * U : k * U + U] + sr[u].astype(F32)

    sums = Scatter(N, b, sc, tb, tr, pieces, st, rt, along_b)
    done = 0
    for_mate(0)
    for i in range(len(pairs)):
        if i + 1 < len(pairs):
            for_mate(i + 1)
        for_me(i)
        while done < N // 2 and (2 * done + 1) < 2 * (i + 1):
            if done == i:
                sums.step(done)
                done += 1
            else:
                break
    while later:
        more()
    while done < N // 2:
        sums.step(done)
        done += 1
    from_mate(xs_ring)
    bo = [jnp.sum(v.astype(F32), axis=0, keepdims=True) for v in (gg[pl.ds(0, N)].reshape(M, HF), gy[...])]
    bo_ref[...] = jnp.concatenate(bo, axis=1).reshape(bo_ref.shape)
    put(bo_ref, bo_hbm)
    bi_ref[...] = jnp.sum(act[...].reshape(M, H).astype(F32), axis=0, keepdims=True).reshape(bi_ref.shape)
    put(bi_ref, bi_hbm)
    for h in range(2):
        wi[h] = tn(ii[pl.ds(h * N, N)].reshape(M, HF), actz[h].reshape(M, H)).astype(BF16)
    put(wi, wi_hbm)

    total = sums.result().astype(BF16)
    stack = jnp.concatenate([total[:, j * W : (j + 1) * W] for j in range(STEPS)], axis=0)
    fb[...] = nn(fold[...], stack).astype(BF16).reshape(2 * N, 16, W)
    slot = c * N + a
    qq[slot] = fb[2 * a + c]
    rcopy(fb.at[2 * a + 1 - c], qq.at[slot], sq.at[0], rq.at[0], mate).start()

    def last(d, _):
        aa = lax.rem(a + d, N)
        for cc in range(2):
            rcopy(fb.at[2 * aa + cc], qq.at[slot], sq.at[0], rq.at[0], adev(aa, cc)).start()
        return 0

    lax.fori_loop(1, N, last, 0)
    got(qq.at[pl.ds(0, 2 * N - 1)], rq.at[0])
    for h in range(2):
        rows = jnp.sum(qq[pl.ds(h * N, N)].astype(F32), axis=0)
        for j in range(STEPS):
            at = h * HF + j * W
            ig_ref[:, at : at + W] = rows[T * j : T * j + T].astype(BF16)
    put(ig_ref, ig_hbm)

    for k in range(2):
        sent(rb.at[k, pl.ds(0, 2 * N - 1)], s1.at[k])
    sent(pre.at[pl.ds(0, X - 1)], s_pre.at[0])
    sent(gg.at[pl.ds(0, 2 * N - 1)], sg.at[0])
    sent(ii.at[pl.ds(0, 2 * N - 1)], si.at[0])
    sent(pb.at[:, pl.ds(0, X - 1)], sp.at[0])
    sent(act.at[pl.ds(0, X - 1)], sa.at[0])
    sent(sx, ss.at[0])
    sent(tb.at[pl.ds(0, N - 1)], st.at[0])
    sent(qq.at[pl.ds(0, 2 * N - 1)], sq.at[0])
    for copy in stores:
        copy.wait()


def finish(*refs):
    srcs, dsts, held, sem = refs[:5], refs[5:10], refs[10:15], refs[15]
    moves = []
    for src, dst, mid in zip(srcs, dsts, held):
        cuts = 4 if len(src.shape) == 2 and src.shape[0] > 64 else 1
        rows = src.shape[0] // cuts
        for k in range(cuts):
            piece = pl.ds(k * rows, rows)
            one, two, three = (r.at[piece] if cuts > 1 else r for r in (src, mid, dst))
            n = 2 * len(moves)
            moves.append((pltpu.make_async_copy(one, two, sem.at[n]), pltpu.make_async_copy(two, three, sem.at[n + 1])))
            moves[-1][0].start()
    for load, store in moves:
        load.wait()
        store.start()
    for load, store in moves:
        store.wait()


def tables(n, u):
    m = n * u
    q = 2 * T
    r = np.arange(m)
    swap = np.zeros((m, m), np.float32)
    swap[r, ((r % u) // q) * u + (r // u) * q + r % q] = 1
    fold = np.zeros((2 * n * 16, STEPS * u), np.float32)
    for j in range(STEPS):
        for t in range(u):
            fold[(t // T) * 16 + T * j + t % T, j * u + t] = 1
    return swap, fold.T, fold


def make_body(X, N, zl_n):
    U = 2 * N * T
    M = N * U

    def body(inputs, pre_act, w_in, w_out, out_grad):
        F, H = w_in.shape
        W = F // (2 * STEPS)
        HF = F // 2
        RB = M // X
        pieces = tuple((at, U // 5) for at in range(0, U, U // 5))
        np_ = len(pieces)
        cfg = {"N": N, "X": X, "ZL": zl_n, "H": H, "W": W, "pieces": pieces}
        consts = [jnp.asarray(t, BF16) for t in tables(N, U)]
        held = [pltpu.VMEM(s, t) for s, t in (((T, F), BF16), ((F, H), BF16), ((H,), F32), ((H, F), BF16), ((F,), F32))]
        hbm = pl.BlockSpec(memory_space=pltpu.HBM)
        dma = pltpu.SemaphoreType.DMA
        outs = pl.pallas_call(
            functools.partial(kernel, cfg),
            out_shape=(
                jax.ShapeDtypeStruct((T, F), BF16),
                jax.ShapeDtypeStruct((2, HF, H), BF16),
                jax.ShapeDtypeStruct((H,), F32),
                jax.ShapeDtypeStruct((H, F), BF16),
                jax.ShapeDtypeStruct((F,), F32),
            ),
            in_specs=[hbm] * 8,
            out_specs=(hbm,) * 5,
            scratch_shapes=[
                pltpu.VMEM(inputs.shape, BF16),
                pltpu.VMEM(out_grad.shape, BF16),
                pltpu.VMEM((T, F), BF16),
                pltpu.VMEM((2, HF, H), BF16),
                pltpu.VMEM((H,), F32),
                pltpu.VMEM((H, F), BF16),
                pltpu.VMEM((F,), F32),
                pltpu.VMEM((2, HF, H), BF16),
                pltpu.VMEM((H, F), BF16),
                pltpu.VMEM(consts[0].shape, BF16),
                pltpu.VMEM(consts[1].shape, BF16),
                pltpu.VMEM(consts[2].shape, BF16),
                pltpu.VMEM((2, 2, 16, W), BF16),
                pltpu.VMEM((2, 2 * N, 16, W), BF16),
                pltpu.VMEM((2 * N, U, HF), BF16),
                pltpu.VMEM((2 * N, U, HF), BF16),
                pltpu.VMEM((M, HF), BF16),
                pltpu.VMEM((X, RB, H), BF16),
                pltpu.VMEM((M, H), F32),
                pltpu.VMEM((M, H), F32),
                pltpu.VMEM((CHUNKS, X, RB // CHUNKS, H), BF16),
                pltpu.VMEM((CHUNKS, X, RB // CHUNKS, H), BF16),
                pltpu.VMEM((X, RB, H), BF16),
                pltpu.VMEM((2, N, U, H), BF16),
                pltpu.VMEM((N, U, HF), BF16),
                pltpu.VMEM((N, U, HF), BF16),
                pltpu.VMEM((N, U, HF), F32),
                pltpu.VMEM((N, U, HF), BF16),
                pltpu.VMEM((N, U, HF), BF16),
                pltpu.VMEM((2 * N, 16, W), BF16),
                pltpu.VMEM((2 * N, 16, W), BF16),
                dma((8,)), dma((5,)),
                dma((1,)), dma((X,)),
                dma((2,)), dma((2,)),
                dma((1,)), dma((2 * N * np_,)),
                dma((1,)), dma((2 * N * np_,)),
                dma((1,)), dma((CHUNKS,)),
                dma((1,)), dma((1,)),
                dma((1,)), dma((N,)),
                dma((1,)), dma((N * np_,)),
                dma((1,)), dma((1,)),
            ],
            compiler_params=pltpu.CompilerParams(
                collective_id=0, has_side_effects=True, vmem_limit_bytes=VM
            ),
        )(inputs, pre_act, w_in.reshape(2, HF, H), w_out, out_grad, *consts)
        ig, wi, bi, wo, bo = outs
        return pl.pallas_call(
            finish,
            out_shape=(
                jax.ShapeDtypeStruct((T, F), BF16),
                jax.ShapeDtypeStruct((F, H), BF16),
                jax.ShapeDtypeStruct((H,), F32),
                jax.ShapeDtypeStruct((H, F), BF16),
                jax.ShapeDtypeStruct((F,), F32),
            ),
            in_specs=[hbm] * 5,
            out_specs=(hbm,) * 5,
            scratch_shapes=[*held, dma((22,))],
            compiler_params=pltpu.CompilerParams(vmem_limit_bytes=VM),
        )(ig, wi.reshape(F, H), bi, wo, bo)

    return body


def solution(mesh):
    zl_n = mesh.shape["col"] // 2
    body = make_body(mesh.shape["row"], math.isqrt(mesh.shape["tok"] * zl_n), zl_n)
    return jax.shard_map(
        body,
        mesh=mesh,
        in_specs=(
            P("tok", "row"),
            P("row", ("tok", "col")),
            P("row", ("tok", "col")),
            P(("tok", "col"), "row"),
            P(("tok", "col"), "row"),
        ),
        out_specs=(
            P(("tok", "col"), "row"),
            P("row", ("tok", "col")),
            P(("tok", "col")),
            P(("tok", "col"), "row"),
            P("row"),
        ),
        check_vma=False,
    )
```

```python
import functools
import math

import jax
import jax.numpy as jnp
import numpy as np
from jax import lax
from jax.experimental import pallas as pl
from jax.experimental.pallas import tpu as pltpu
from jax.sharding import PartitionSpec as P

MESH = pl.DeviceIdType.MESH
F32 = jnp.float32
BF16 = jnp.bfloat16
root_two_pi = math.sqrt(2.0 / math.pi)
T = 5
ZL = 4
CHUNKS = 2
VM = 60 * 2**20
STEPS = 3


def gelu_parts(values):
    cubic = values * values * values
    inner = root_two_pi * (values + 0.044715 * cubic)
    tangent = jnp.tanh(inner)
    result = 0.5 * values * (1.0 + tangent)
    slope = 0.5 * (1.0 + tangent) + 0.5 * values * (1.0 - tangent * tangent) * root_two_pi * (
        1.0 + 3.0 * 0.044715 * values * values
    )
    return (result, slope)


def nt(a, b):
    return lax.dot_general(a, b, (((1,), (1,)), ((), ())), preferred_element_type=F32)


def tn(a, b):
    return lax.dot_general(a, b, (((0,), (0,)), ((), ())), preferred_element_type=F32)


def nn(a, b):
    return lax.dot_general(a, b, (((1,), (0,)), ((), ())), preferred_element_type=F32)


class Gather:
    def __init__(self, n, me, buf, slot, pieces, ssem, rsem, msem, send):
        self.n, self.me, self.buf, self.slot, self.pieces = n, me, buf, slot, pieces
        self.ssem, self.rsem, self.msem, self.send = ssem, rsem, msem, send
        self.all = range(len(pieces))

    def piece(self, unit, p):
        at, size = self.pieces[p]
        return self.buf.at[self.slot(unit), pl.ds(at, size)], self.rsem.at[self.slot(unit) * len(self.pieces) + p]

    def push(self, unit, p, to):
        ref, sem = self.piece(unit, p)
        self.send(ref, ref, self.ssem.at[0], sem if to else self.msem.at[0], to).start()

    def far(self, way, p):
        return (p < (len(self.pieces) + 1) // 2) == (way > 0)

    def start(self):
        for hop in (2, 1):
            for p in self.all:
                for way in (1, -1):
                    self.push(self.me, p, way * hop)
        for p in self.all:
            self.push(self.me, p, 0)

    def step(self, k):
        for p in self.all:
            for way in (1, -1):
                if k < 4 or self.far(way, p):
                    unit = lax.rem(self.me - way * k + self.n, self.n)
                    ref, sem = self.piece(unit, p)
                    self.send(ref, ref, sem, sem, 0).wait_recv()
                    if k == 2:
                        if self.far(way, p):
                            self.push(unit, p, 2 * way)
                        self.push(unit, p, way)
                    self.push(unit, p, 0)


class Scatter:
    def __init__(self, n, me, own, out, land, pieces, ssem, rsem, send):
        self.n, self.me, self.own, self.out, self.land, self.pieces = n, me, own, out, land, pieces
        self.ssem, self.rsem, self.send = ssem, rsem, send
        self.all = range(len(pieces))

    def far(self, way, p):
        return (p < (len(self.pieces) + 1) // 2) == (way > 0)

    def place(self, way, s, p):
        at = (0 if way > 0 else 4) + s
        rows = pl.ds(*self.pieces[p])
        return self.out.at[at, rows], self.land.at[at, rows], self.rsem.at[at * len(self.pieces) + p]

    def arrived(self, way, s, p):
        _, land, sem = self.place(way, s, p)
        self.send(land, land, sem, sem, 0).wait_recv()
        return land[...].astype(F32)

    def step(self, s, way):
        unit = lax.rem(self.me + way * (4, 3, 1, 2)[s] + self.n, self.n)
        for p in self.all:
            if s or self.far(way, p):
                value = self.own[unit, pl.ds(*self.pieces[p])]
                if s == 3:
                    value = value + self.arrived(way, 1, p)
                    if self.far(way, p):
                        value = value + self.arrived(way, 0, p)
                out, land, sem = self.place(way, s, p)
                out[...] = value.astype(BF16)
                self.send(out, land, self.ssem.at[0], sem, way * (2, 1, 1, 2)[s]).start()

    def result(self):
        rows = []
        for p in self.all:
            value = self.own[self.me, pl.ds(*self.pieces[p])]
            for s in (2, 3):
                for way in (1, -1):
                    value = value + self.arrived(way, s, p)
            rows.append(value)
        return jnp.concatenate(rows, axis=0)


def kernel(
    cfg,
    x_hbm, pre_hbm, w_in_hbm, w_out_hbm, og_hbm, swap_hbm, unfold_hbm, fold_hbm,
    ig_hbm, wi_hbm, bi_hbm, wo_hbm, bo_hbm,
    x_ref, og_ref, ig_ref, wi, bi_ref, wo, bo_ref,
    w_in, w_out, swap, unfold, fold, sb, rb, gg, ii, gy, pre, hid, slope, pb, pr, act, actz, sx, sr, sc, tb, tr,
    fb, qq,
    loc, outs, s_pre, r_pre, s1, r1, sg, rg, mg, si, ri, mi, sp, rp, sa, ra, ss, rs, st, rt, sq, rq,
):
    N, X, zl_n = cfg["N"], cfg["X"], cfg["ZL"]
    U = 2 * N * T
    H = cfg["H"]
    W = cfg["W"]
    HF = STEPS * W
    M = N * U
    RB = M // X
    UR = RB // U
    TK = 2 * zl_n * T

    tok, x, col = lax.axis_index("tok"), lax.axis_index("row"), lax.axis_index("col")
    y, c = lax.rem(tok, N), lax.rem(col, 2)
    z = (tok // N) * zl_n + col // 2
    b = y + c * (z - y)
    a = z + c * (y - z)

    def dev(yy, zz, cc, xx=x):
        return ((zz // zl_n) * N + yy, xx, lax.rem(zz, zl_n) * 2 + cc)

    def bdev(bb):
        return dev(y + (1 - c) * (bb - y), z + c * (bb - z), c)

    def adev(aa, cc):
        return dev(y + c * (aa - y), z + (1 - c) * (aa - z), cc)

    def xdev(xx):
        return dev(y, z, c, xx)

    mate = dev(y, z, 1 - c)

    def rcopy(src, dst, ssem, rsem, to):
        return pltpu.make_async_remote_copy(
            src_ref=src, dst_ref=dst, send_sem=ssem, recv_sem=rsem, device_id=to, device_id_type=MESH
        )

    def along_b(src, dst, ssem, rsem, way):
        to = mate if way == 0 else bdev(lax.rem(b + way + N, N))
        return rcopy(src, dst, ssem, rsem, to)

    def along_x(src, dst, ssem, rsem, way):
        return rcopy(src, dst, ssem, rsem, xdev(lax.rem(x + way + X, X)))

    def got(dst, rsem):
        rcopy(dst, dst, rsem, rsem, mate).wait_recv()

    def sent(src, ssem):
        rcopy(src, src, ssem, ssem, mate).wait_send()

    loads = [
        pltpu.make_async_copy(pre_hbm, pre.at[x], loc.at[0]),
        pltpu.make_async_copy(unfold_hbm, unfold, loc.at[1]),
        pltpu.make_async_copy(swap_hbm, swap, loc.at[2]),
        pltpu.make_async_copy(w_out_hbm, w_out, loc.at[3]),
        pltpu.make_async_copy(w_in_hbm, w_in, loc.at[4]),
        pltpu.make_async_copy(fold_hbm, fold, loc.at[5]),
    ]
    tokens = (pltpu.make_async_copy(og_hbm, og_ref, loc.at[6]), pltpu.make_async_copy(x_hbm, x_ref, loc.at[7]))
    for load in tokens:
        load.start()

    stores = []

    def put(src, dst):
        stores.append(pltpu.make_async_copy(src, dst, outs.at[len(stores)]))
        stores[-1].start()

    bar = pltpu.get_barrier_semaphore()

    def greet(yy, zz, cc, xx=x):
        pl.semaphore_signal(bar, inc=1, device_id=dev(yy, zz, cc, xx), device_id_type=MESH)

    greet(y, z, 1 - c)
    for d in range(1, X):
        greet(y, z, c, lax.rem(x + d, X))

    def greet_step(d, _):
        yy, zz = lax.rem(y + d, N), lax.rem(z + d, N)
        for cc in range(2):
            greet(yy, z, cc)
            greet(y, zz, cc)
        return 0

    lax.fori_loop(1, N, greet_step, 0)

    for load in loads:
        load.start()

    for load in tokens:
        load.wait()
    og = og_ref[...].astype(F32)
    xall = x_ref[...].astype(F32)
    xs = xall[0:T]
    for k in range(1, 2 * zl_n):
        xs = jnp.where(col == k, xall[T * k : T * k + T], xs)
    pad = jnp.zeros((1, W), F32)
    for k, v in enumerate((og, xs)):
        for h in range(2):
            rows = [v[:, h * HF + j * W : h * HF + (j + 1) * W] for j in range(STEPS)] + [pad]
            sb[k, h] = jnp.concatenate(rows, axis=0).astype(BF16)

    pl.semaphore_wait(bar, 1 + (X - 1) + 4 * (N - 1))

    def small_phase(k):
        @pl.when(c == 0)
        def _():
            rb[k, 2 * z] = sb[k, 0]
            rcopy(sb.at[k, 1], rb.at[k, 2 * y], s1.at[k], r1.at[k], mate).start()

        @pl.when(c == 1)
        def _():
            rb[k, 2 * y + 1] = sb[k, 1]
            rcopy(sb.at[k, 0], rb.at[k, 2 * z + 1], s1.at[k], r1.at[k], mate).start()

        def small(d, _):
            yy, zz = lax.rem(y + d, N), lax.rem(z + d, N)
            rcopy(sb.at[k, 0], rb.at[k, 2 * z + c], s1.at[k], r1.at[k], dev(y, zz, 0)).start()
            rcopy(sb.at[k, 1], rb.at[k, 2 * y + c], s1.at[k], r1.at[k], dev(yy, z, 1)).start()
            return 0

        lax.fori_loop(1, N, small, 0)

    def unit_of(k, buf):
        got(rb.at[k, pl.ds(0, 2 * N - 1)], r1.at[k])
        unit = nn(unfold[...], rb[k].reshape(2 * N * 16, W)).astype(BF16)
        for j in range(STEPS):
            buf[c * N + b, :, j * W : (j + 1) * W] = unit[j * U : j * U + U]

    small_phase(0)

    for d in range(1, X):
        rcopy(pre_hbm, pre.at[x], s_pre.at[0], r_pre.at[x], xdev(lax.rem(x + d, X))).start()

    def gelu_block(r):
        for q in range(RB // TK):
            g = r * (RB // TK) + q
            zh, yy = g // N, lax.rem(g, N)
            rows = pl.ds(pl.multiple_of(yy * U + zh * TK, 8), TK)
            result, grade = gelu_parts(pre[r].astype(F32)[q * TK : q * TK + TK])
            hid[rows] = result
            slope[rows] = grade

    loads[0].wait()
    gelu_block(x)
    loads[1].wait()
    pieces = cfg["pieces"]
    grads = Gather(N, b, gg, lambda u: c * N + u, pieces, sg, rg, mg, along_b)
    xs_ring = Gather(N, b, ii, lambda u: c * N + u, pieces, si, ri, mi, along_b)
    unit_of(0, gg)
    grads.start()
    small_phase(1)

    def from_mate(ring):
        got(ring.buf.at[pl.ds((1 - c) * N, N)], ring.msem.at[0])

    for k in range(1, N // 2 + 1):
        grads.step(k)
        if k < X:
            r = lax.rem(x + k, X)
            got(pre.at[r], r_pre.at[r])
            gelu_block(r)
    for k in range(N // 2 + 1, X):
        r = lax.rem(x + k, X)
        got(pre.at[r], r_pre.at[r])
        gelu_block(r)
    for load in loads[2:]:
        load.wait()
    from_mate(grads)

    def part(r):
        g1 = gg[pl.ds(N, N)].reshape(M, HF)
        mine = pl.ds(pl.multiple_of(r * RB, 16), RB)
        g1y = nn(swap[mine], g1).astype(BF16)
        gy[mine] = g1y
        g0 = gg[pl.ds(r * UR, UR)].reshape(RB, HF)
        return nt(g0, w_out[:, :HF]) + nt(g1y, w_out[:, HF:])

    def steps(n, me):
        return [n // 2] + [v for s in range(1, n // 2) for v in (n // 2 - s, n // 2 + s)] + [0]

    later = list(range(1, N // 2 + 1))

    def more():
        if later:
            xs_ring.step(later.pop(0))

    CH = RB // CHUNKS
    for v in steps(X, x)[:-1]:
        r = lax.rem(x + v, X)
        value = part(r).astype(BF16)
        for q in range(CHUNKS):
            pb[q, r] = value[q * CH : q * CH + CH]
            rcopy(pb.at[q, r], pr.at[q, x], sp.at[0], rp.at[q], xdev(r)).start()
    mine = part(x)

    unit_of(1, ii)
    xs_ring.start()
    hidden = hid[...].astype(BF16)
    wo[:, :HF] = tn(hidden, gg[pl.ds(0, N)].reshape(M, HF)).astype(BF16)
    for q in range(CHUNKS):
        got(pr.at[q, pl.ds(0, X - 1)], rp.at[q])
        total = mine[q * CH : q * CH + CH]
        for v in range(1, X):
            total = total + pr[q, lax.rem(x + v, X)].astype(F32)
        rows = pl.ds(pl.multiple_of(x * RB + q * CH, 16), CH)
        act[x, q * CH : q * CH + CH] = (total * slope[rows]).astype(BF16)
        piece = act.at[x, pl.ds(q * CH, CH)]
        for v in steps(X, x)[:-1]:
            rcopy(piece, piece, sa.at[0], ra.at[0], xdev(lax.rem(x + v, X))).start()
    more()
    wo[:, HF:] = tn(hidden, gy[...]).astype(BF16)
    put(wo, wo_hbm)
    more()
    got(act.at[pl.ds(0, X - 1)], ra.at[0])
    acty = act[...].reshape(M, H)
    actz[0] = acty.reshape(N, U, H)
    actz[1] = nn(swap[...], acty).astype(BF16).reshape(N, U, H)

    mate_b = z + c * (y - z)
    order = steps(N, b)
    pairs = [order[i : i + 2] for i in range(0, N, 2)]

    def product(h, base, pair):
        units = [lax.rem(base + v, N) for v in pair]
        rows = jnp.concatenate([actz[h, u] for u in units], axis=0)
        return units, nt(rows, w_in[h])

    def for_mate(i):
        units, value = product(1 - c, mate_b, pairs[i])
        for k, u in enumerate(units):
            sx[u] = value[k * U : k * U + U].astype(BF16)
            rcopy(sx.at[u], sr.at[u], ss.at[0], rs.at[u], mate).start()

    def for_me(i):
        units, value = product(c, b, pairs[i])
        for k, u in enumerate(units):
            got(sr.at[u], rs.at[u])
            sc[u] = value[k * U : k * U + U] + sr[u].astype(F32)

    sums = Scatter(N, b, sc, tb, tr, pieces, st, rt, along_b)
    for_mate(0)
    for_mate(1)
    for_me(0)
    for s, way in ((0, 1), (0, -1), (1, 1)):
        sums.step(s, way)
    for_mate(2)
    for_me(1)
    sums.step(1, -1)
    for_mate(3)
    for_me(2)
    sums.step(2, 1)
    for_me(3)
    sums.step(2, -1)
    sums.step(3, 1)
    sums.step(3, -1)
    while later:
        more()
    from_mate(xs_ring)
    bo = [jnp.sum(v.astype(F32), axis=0, keepdims=True) for v in (gg[pl.ds(0, N)].reshape(M, HF), gy[...])]
    bo_ref[...] = jnp.concatenate(bo, axis=1).reshape(bo_ref.shape)
    put(bo_ref, bo_hbm)
    bi_ref[...] = jnp.sum(act[...].reshape(M, H).astype(F32), axis=0, keepdims=True).reshape(bi_ref.shape)
    put(bi_ref, bi_hbm)
    for h in range(2):
        wi[h] = tn(ii[pl.ds(h * N, N)].reshape(M, HF), actz[h].reshape(M, H)).astype(BF16)
    put(wi, wi_hbm)

    total = sums.result().astype(BF16)
    stack = jnp.concatenate([total[:, j * W : (j + 1) * W] for j in range(STEPS)], axis=0)
    fb[...] = nn(fold[...], stack).astype(BF16).reshape(2 * N, 16, W)
    slot = c * N + a
    qq[slot] = fb[2 * a + c]
    rcopy(fb.at[2 * a + 1 - c], qq.at[slot], sq.at[0], rq.at[0], mate).start()

    def last(d, _):
        aa = lax.rem(a + d, N)
        for cc in range(2):
            rcopy(fb.at[2 * aa + cc], qq.at[slot], sq.at[0], rq.at[0], adev(aa, cc)).start()
        return 0

    lax.fori_loop(1, N, last, 0)
    got(qq.at[pl.ds(0, 2 * N - 1)], rq.at[0])
    for h in range(2):
        rows = jnp.sum(qq[pl.ds(h * N, N)].astype(F32), axis=0)
        for j in range(STEPS):
            at = h * HF + j * W
            ig_ref[:, at : at + W] = rows[T * j : T * j + T].astype(BF16)
    put(ig_ref, ig_hbm)

    for k in range(2):
        sent(rb.at[k, pl.ds(0, 2 * N - 1)], s1.at[k])
    sent(pre.at[pl.ds(0, X - 1)], s_pre.at[0])
    sent(gg.at[pl.ds(0, 2 * N - 1)], sg.at[0])
    sent(ii.at[pl.ds(0, 2 * N - 1)], si.at[0])
    sent(pb.at[:, pl.ds(0, X - 1)], sp.at[0])
    sent(act.at[pl.ds(0, X - 1)], sa.at[0])
    sent(sx, ss.at[0])
    sent(tb.at[pl.ds(0, N - 1)], st.at[0])
    sent(qq.at[pl.ds(0, 2 * N - 1)], sq.at[0])
    for copy in stores:
        copy.wait()


def finish(*refs):
    srcs, dsts, held, sem = refs[:5], refs[5:10], refs[10:15], refs[15]
    moves = []
    for src, dst, mid in zip(srcs, dsts, held):
        cuts = 4 if len(src.shape) == 2 and src.shape[0] > 64 else 1
        rows = src.shape[0] // cuts
        for k in range(cuts):
            piece = pl.ds(k * rows, rows)
            one, two, three = (r.at[piece] if cuts > 1 else r for r in (src, mid, dst))
            n = 2 * len(moves)
            moves.append((pltpu.make_async_copy(one, two, sem.at[n]), pltpu.make_async_copy(two, three, sem.at[n + 1])))
            moves[-1][0].start()
    for load, store in moves:
        load.wait()
        store.start()
    for load, store in moves:
        store.wait()


def tables(n, u):
    m = n * u
    q = 2 * T
    r = np.arange(m)
    swap = np.zeros((m, m), np.float32)
    swap[r, ((r % u) // q) * u + (r // u) * q + r % q] = 1
    fold = np.zeros((2 * n * 16, STEPS * u), np.float32)
    for j in range(STEPS):
        for t in range(u):
            fold[(t // T) * 16 + T * j + t % T, j * u + t] = 1
    return swap, fold.T, fold


def make_body(X, N, zl_n):
    U = 2 * N * T
    M = N * U

    def body(inputs, pre_act, w_in, w_out, out_grad):
        F, H = w_in.shape
        W = F // (2 * STEPS)
        HF = F // 2
        RB = M // X
        pieces = ((0, U * 3 // 5), (U * 3 // 5, U * 2 // 5))
        np_ = len(pieces)
        cfg = {"N": N, "X": X, "ZL": zl_n, "H": H, "W": W, "pieces": pieces}
        consts = [jnp.asarray(t, BF16) for t in tables(N, U)]
        held = [pltpu.VMEM(s, t) for s, t in (((T, F), BF16), ((F, H), BF16), ((H,), F32), ((H, F), BF16), ((F,), F32))]
        hbm = pl.BlockSpec(memory_space=pltpu.HBM)
        dma = pltpu.SemaphoreType.DMA
        outs = pl.pallas_call(
            functools.partial(kernel, cfg),
            out_shape=(
                jax.ShapeDtypeStruct((T, F), BF16),
                jax.ShapeDtypeStruct((2, HF, H), BF16),
                jax.ShapeDtypeStruct((H,), F32),
                jax.ShapeDtypeStruct((H, F), BF16),
                jax.ShapeDtypeStruct((F,), F32),
            ),
            in_specs=[hbm] * 8,
            out_specs=(hbm,) * 5,
            scratch_shapes=[
                pltpu.VMEM(inputs.shape, BF16),
                pltpu.VMEM(out_grad.shape, BF16),
                pltpu.VMEM((T, F), BF16),
                pltpu.VMEM((2, HF, H), BF16),
                pltpu.VMEM((H,), F32),
                pltpu.VMEM((H, F), BF16),
                pltpu.VMEM((F,), F32),
                pltpu.VMEM((2, HF, H), BF16),
                pltpu.VMEM((H, F), BF16),
                pltpu.VMEM(consts[0].shape, BF16),
                pltpu.VMEM(consts[1].shape, BF16),
                pltpu.VMEM(consts[2].shape, BF16),
                pltpu.VMEM((2, 2, 16, W), BF16),
                pltpu.VMEM((2, 2 * N, 16, W), BF16),
                pltpu.VMEM((2 * N, U, HF), BF16),
                pltpu.VMEM((2 * N, U, HF), BF16),
                pltpu.VMEM((M, HF), BF16),
                pltpu.VMEM((X, RB, H), BF16),
                pltpu.VMEM((M, H), F32),
                pltpu.VMEM((M, H), F32),
                pltpu.VMEM((CHUNKS, X, RB // CHUNKS, H), BF16),
                pltpu.VMEM((CHUNKS, X, RB // CHUNKS, H), BF16),
                pltpu.VMEM((X, RB, H), BF16),
                pltpu.VMEM((2, N, U, H), BF16),
                pltpu.VMEM((N, U, HF), BF16),
                pltpu.VMEM((N, U, HF), BF16),
                pltpu.VMEM((N, U, HF), F32),
                pltpu.VMEM((N, U, HF), BF16),
                pltpu.VMEM((N, U, HF), BF16),
                pltpu.VMEM((2 * N, 16, W), BF16),
                pltpu.VMEM((2 * N, 16, W), BF16),
                dma((8,)), dma((5,)),
                dma((1,)), dma((X,)),
                dma((2,)), dma((2,)),
                dma((1,)), dma((2 * N * np_,)), dma((1,)),
                dma((1,)), dma((2 * N * np_,)), dma((1,)),
                dma((1,)), dma((CHUNKS,)),
                dma((1,)), dma((1,)),
                dma((1,)), dma((N,)),
                dma((1,)), dma((N * np_,)),
                dma((1,)), dma((1,)),
            ],
            compiler_params=pltpu.CompilerParams(
                collective_id=0, has_side_effects=True, vmem_limit_bytes=VM
            ),
        )(inputs, pre_act, w_in.reshape(2, HF, H), w_out, out_grad, *consts)
        ig, wi, bi, wo, bo = outs
        return pl.pallas_call(
            finish,
            out_shape=(
                jax.ShapeDtypeStruct((T, F), BF16),
                jax.ShapeDtypeStruct((F, H), BF16),
                jax.ShapeDtypeStruct((H,), F32),
                jax.ShapeDtypeStruct((H, F), BF16),
                jax.ShapeDtypeStruct((F,), F32),
            ),
            in_specs=[hbm] * 5,
            out_specs=(hbm,) * 5,
            scratch_shapes=[*held, dma((22,))],
            compiler_params=pltpu.CompilerParams(vmem_limit_bytes=VM),
        )(ig, wi.reshape(F, H), bi, wo, bo)

    return body


def solution(mesh):
    zl_n = mesh.shape["col"] // 2
    body = make_body(mesh.shape["row"], math.isqrt(mesh.shape["tok"] * zl_n), zl_n)
    return jax.shard_map(
        body,
        mesh=mesh,
        in_specs=(
            P("tok", "row"),
            P("row", ("tok", "col")),
            P("row", ("tok", "col")),
            P(("tok", "col"), "row"),
            P(("tok", "col"), "row"),
        ),
        out_specs=(
            P(("tok", "col"), "row"),
            P("row", ("tok", "col")),
            P(("tok", "col")),
            P(("tok", "col"), "row"),
            P("row"),
        ),
        check_vma=False,
    )
```
